128 devices in a mesh: pipe: 8 (over x_lo, y), tensor: 8 (over z, core), dp: 2 (over x_hi).
Axes of the slice: x: 4 (x_hi: 2, x_lo: 2; x = x_hi * 2 + x_lo), y: 4, z: 4, core: 2. Of those that a mesh axis runs over, the one named last changes fastest.
Arguments:
- inputs: bfloat16 [2, 256, 2560], P(None, 'dp'), may hold values from -60 to 60
- cotangent: bfloat16 [2, 256, 2560], P(None, 'dp'), may hold values from -6 to 6
- lengths: int32 [2, 2, 4], P(None, 'dp'), may hold values from 1 to 64, 128 in all within a row
- down_qkv: bfloat16 [8, 2560, 3, 3072], P('pipe', None, None, 'tensor'), may hold values from -6 to 6
- down_out: bfloat16 [8, 2560, 3072], P('pipe', None, 'tensor'), may hold values from -0.109375 to 0.109375
- down_gain: bfloat16 [8, 2560], P('pipe'), may hold values from 0.099609375 to 1.8984375
- up_qkv: bfloat16 [8, 2560, 3, 3072], P('pipe', None, None, 'tensor'), may hold values from -6 to 6
- up_out: bfloat16 [8, 2560, 3072], P('pipe', None, 'tensor'), may hold values from -0.109375 to 0.109375
- up_gain: bfloat16 [8, 2560], P('pipe'), may hold values from 0.099609375 to 1.8984375
Outputs:
- grad_qkv: float32 [8, 2560, 3, 3072], P('pipe', 'dp', None, 'tensor')
- grad_out: float32 [8, 2560, 3072], P('pipe', 'dp', 'tensor')
The draws below stay inside these ranges and needn't reach their ends.
Inputs may be any that keep to these rules, and one draw needn't show every extreme that they name: Each row holds 4 document lengths of one micro-batch that sum to 128; the longest is exactly 64.
All inputs are finite; a program needn't handle non-finite values.
Results may differ from the reference program's by a relative error of at most 0.039.
Values may be sent and summed in bfloat16 or wider, within the bound.
No kernel may reach another device: no remote copies, remote signals or barrier semaphores. Data moves between devices by JAX's collectives and lax.ppermute only.
A program may use at most 256 MiB of HBM per device.

```python
import math
import jax
import jax.numpy as jnp
import numpy as np
from jax import lax

D = 2560
HS = 128
TOK = 128
DOCS = 4
SECTIONS = 8
HD = 3072
TOKENS = 256
N_TENSOR = 8
N_DP = 2


def draw_inputs(key, part):
    key = jax.random.fold_in(key, 13)
    noise_key = jax.random.fold_in(key, 0)
    base = jnp.clip(jax.random.normal(noise_key, (2, TOKENS, D), jnp.float32), -6.0, 6.0)
    return base.astype(jnp.bfloat16)


def draw_down_qkv(key, part):
    key = jax.random.fold_in(key, 11)
    base_key = jax.random.fold_in(key, 0)
    base = jnp.clip(jax.random.normal(base_key, (SECTIONS, D, 3, HD), jnp.float32), -6.0, 6.0) * D ** (-0.5)
    return base.astype(jnp.bfloat16)


def draw_up_qkv(key, part):
    key = jax.random.fold_in(key, 12)
    base_key = jax.random.fold_in(key, 0)
    base = jnp.clip(jax.random.normal(base_key, (SECTIONS, D, 3, HD), jnp.float32), -6.0, 6.0) * D ** (-0.5)
    return base.astype(jnp.bfloat16)


def steps_of(own_key, extent, shards, least, largest):
    gain, own = 1.0, jax.random.fold_in(own_key, 6)
    for position, blocks in shards:
        heights = jnp.exp(jax.random.uniform(jax.random.fold_in(own, position), (blocks,), jnp.float32, least / len(shards), largest / len(shards)))
        gain = gain * jnp.repeat(heights, extent[position] // blocks).reshape([-1 if axis == position else 1 for axis in range(len(extent))])
    return gain


def length_profile(amount, total, most, skew):
    portions = [(1 << 20) // math.isqrt(standing ** skew) + 1 for standing in range(2, amount + 1)]
    rest, holding = total - most - (amount - 1), [1] * (amount - 1)
    while rest > 0:
        movable = [i for i in range(amount - 1) if holding[i] < most]
        mass, budget = sum([portions[i] for i in movable]), rest
        for i in movable:
            addition = min(most - holding[i], max(1, budget * portions[i] // mass), rest)
            holding[i] = holding[i] + addition
            rest = rest - addition
    return np.array([most] + holding)


def ragged_sizes(stream_key, number_of, total, reach, skew):
    if number_of == 2:
        one = jax.random.randint(stream_key, (), max(1, total - reach), min(reach, total - 1) + 1)
        return jnp.stack([one, total - one])
    sizes = jnp.asarray(length_profile(number_of, total, reach, skew), jnp.int32)
    pairs = (number_of - 1) // 2
    donor, sink = sizes[1:1 + 2 * pairs:2], sizes[2:2 + 2 * pairs:2]
    room = jnp.minimum(donor - 1, reach - sink)
    shifted = jax.random.randint(jax.random.fold_in(stream_key, 1), (pairs,), 0, 1 << 20) % (room + 1)
    sizes = sizes.at[1:1 + 2 * pairs:2].set(donor - shifted).at[2:2 + 2 * pairs:2].set(sink + shifted)
    return sizes[jax.random.permutation(jax.random.fold_in(stream_key, 2), number_of)]


def gaussian(stream_key, dims, spread, reach, pieces=(), kind=jnp.bfloat16):
    loudness = steps_of(stream_key, dims, pieces, -0.22, 0.18) if pieces else 1.0
    result = jax.random.normal(stream_key, dims, jnp.float32) * spread * loudness
    return jnp.minimum(jnp.maximum(result, -reach), reach).astype(kind)


def setup_inputs(seed: int = 0) -> dict:
    seeds = jax.random.split(jax.random.key(seed), 10)
    inputs = draw_inputs(jax.random.fold_in(seeds[9], 71), 0)
    cotangent = gaussian(seeds[1], (2, TOKENS, D), 1.0, 6.0, ((1, 2),))
    lengths = jax.vmap(lambda own: ragged_sizes(own, DOCS, TOK, TOK // 2, 2))(jax.random.split(seeds[2], 2 * N_DP)).reshape((2, N_DP, DOCS)).astype(jnp.int32)
    down_qkv = draw_down_qkv(jax.random.fold_in(seeds[9], 71), 0)
    down_out = gaussian(seeds[4], (SECTIONS, D, HD), HD ** -0.5, 0.109375, ((0, 8), (2, 8)))
    down_gain = jnp.clip(1.0 + 0.18 * jax.random.normal(seeds[5], (SECTIONS, D), jnp.float32), 0.099609375, 1.8984375).astype(jnp.bfloat16)
    up_qkv = draw_up_qkv(jax.random.fold_in(seeds[9], 71), 0)
    up_out = gaussian(seeds[7], (SECTIONS, D, HD), HD ** -0.5, 0.109375, ((0, 8), (2, 8)))
    up_gain = jnp.clip(1.0 + 0.18 * jax.random.normal(seeds[8], (SECTIONS, D), jnp.float32), 0.099609375, 1.8984375).astype(jnp.bfloat16)
    return dict(inputs=inputs, cotangent=cotangent, lengths=lengths, down_qkv=down_qkv, down_out=down_out, down_gain=down_gain, up_qkv=up_qkv, up_out=up_out, up_gain=up_gain)


norm_epsilon = 1e-05

def doc_mask(doc_lengths, row_count):
    doc_ends = jnp.cumsum(doc_lengths).astype(jnp.int32)
    places = jnp.arange(row_count, dtype=jnp.int32)
    segment = lax.optimization_barrier(jnp.sum((places[:, None] >= doc_ends[None, :]).astype(jnp.int32), axis=1))
    return (segment[:, None] == segment[None, :]) & (places[None, :] <= places[:, None])

def normalize(section_input, gain_vector):
    floated = section_input.astype(jnp.float32)
    centred = floated - lax.optimization_barrier(jnp.mean(floated, axis=-1, keepdims=True))
    inv_scale = lax.rsqrt(lax.optimization_barrier(jnp.mean(centred * centred, axis=-1, keepdims=True)) + norm_epsilon)
    normed = (centred * inv_scale * gain_vector).astype(jnp.bfloat16)
    return (normed, centred, inv_scale)

def rounded(values_in):
    return lax.optimization_barrier(values_in.astype(jnp.bfloat16)).astype(jnp.float32)

def attend(normed, group_cols, allowed):
    row_count = normed.shape[0]
    group_width = group_cols.shape[1] // 3
    heads_here = group_width // HS
    factor = HS ** (-0.5)
    projected = jnp.dot(normed, group_cols, preferred_element_type=jnp.float32).astype(jnp.bfloat16)
    projected = projected.reshape(row_count, 3, heads_here, HS)
    queries = projected[:, 0]
    key_rows = projected[:, 1]
    values = projected[:, 2]
    scores = jnp.einsum('thd,shd->hts', queries.astype(jnp.float32), key_rows.astype(jnp.float32)) * factor
    scores = jnp.where(allowed[None], scores, -1e+30)
    highest = lax.optimization_barrier(jnp.max(scores, axis=-1, keepdims=True))
    raised = jnp.exp(scores - highest)
    probability = raised / lax.optimization_barrier(jnp.sum(raised, axis=-1, keepdims=True))
    weights = probability.astype(jnp.bfloat16)
    context = jnp.einsum('hts,shd->thd', weights.astype(jnp.float32), values.astype(jnp.float32))
    context = context.astype(jnp.bfloat16).reshape(row_count, group_width)
    return (queries, key_rows, values, probability, weights, context)

def attend_back(out_grad, group_cols, group_out, cached, need_input):
    queries, key_rows, values, probability, weights, context = cached
    row_count = out_grad.shape[0]
    group_width = group_out.shape[1]
    heads_here = group_width // HS
    factor = HS ** (-0.5)
    ctx_grad = jnp.dot(out_grad, group_out, preferred_element_type=jnp.float32).astype(jnp.bfloat16)
    ctx_grad = ctx_grad.reshape(row_count, heads_here, HS)
    prob_grad = jnp.einsum('thd,shd->hts', ctx_grad.astype(jnp.float32), values.astype(jnp.float32))
    inner_sum = lax.optimization_barrier(jnp.sum(probability * prob_grad, axis=-1, keepdims=True))
    score_grad = (probability * (prob_grad - inner_sum) * factor).astype(jnp.bfloat16)
    query_grad = jnp.einsum('hts,shd->thd', score_grad.astype(jnp.float32), key_rows.astype(jnp.float32))
    key_grad = jnp.einsum('hts,thd->shd', score_grad.astype(jnp.float32), queries.astype(jnp.float32))
    value_grad = jnp.einsum('hts,thd->shd', weights.astype(jnp.float32), ctx_grad.astype(jnp.float32))
    qkv_grad = jnp.stack([query_grad, key_grad, value_grad], axis=1).reshape(row_count, 3 * group_width)
    qkv_grad = qkv_grad.astype(jnp.bfloat16)
    if need_input:
        normed_grad = lax.dot_general(qkv_grad, group_cols, (((1,), (1,)), ((), ())), preferred_element_type=jnp.float32)
    else:
        normed_grad = jnp.zeros((row_count, group_cols.shape[0]), jnp.float32)
    return (normed_grad, qkv_grad, context)

def norm_back(normed_grad, centred, inv_scale, gain_vector):
    scaled = normed_grad * gain_vector
    unit_rows = centred * inv_scale
    first_mean = lax.optimization_barrier(jnp.mean(scaled, axis=-1, keepdims=True))
    second_mean = lax.optimization_barrier(jnp.mean(scaled * unit_rows, axis=-1, keepdims=True))
    return inv_scale * (scaled - first_mean - unit_rows * second_mean)

def group_tables(qkv_weight, out_weight, group_index):
    group_width = HD // N_TENSOR
    low = group_index * group_width
    group_cols = qkv_weight[:, :, low:low + group_width].reshape(D, 3 * group_width)
    group_out = out_weight[:, low:low + group_width]
    return (group_cols, group_out)

def section_front(section_input, gain_vector, qkv_weight, out_weight, allowed):
    normed, _, _ = normalize(section_input, gain_vector)
    summed_out = jnp.zeros((TOK, D), jnp.float32)
    for group_index in range(N_TENSOR):
        group_cols, group_out = group_tables(qkv_weight, out_weight, group_index)
        context = attend(normed, group_cols, allowed)[5]
        partial_value = lax.dot_general(context, group_out, (((1,), (1,)), ((), ())), preferred_element_type=jnp.float32)
        summed_out = summed_out + rounded(partial_value)
    return (section_input.astype(jnp.float32) + summed_out).astype(jnp.bfloat16)

def section_back(section_input, out_grad, gain_vector, qkv_weight, out_weight, allowed, need_input):
    normed, centred, inv_scale = normalize(section_input, gain_vector)
    group_width = HD // N_TENSOR
    summed_grad = jnp.zeros((TOK, D), jnp.float32)
    qkv_parts = []
    context_parts = []
    for group_index in range(N_TENSOR):
        group_cols, group_out = group_tables(qkv_weight, out_weight, group_index)
        cached = attend(normed, group_cols, allowed)
        normed_grad, qkv_grad, context = attend_back(out_grad, group_cols, group_out, cached, need_input)
        summed_grad = summed_grad + rounded(normed_grad)
        qkv_parts.append(qkv_grad.reshape(TOK, 3, group_width))
        context_parts.append(context)
    qkv_full = jnp.concatenate(qkv_parts, axis=2)
    context_full = jnp.concatenate(context_parts, axis=1)
    input_grad = out_grad
    if need_input:
        input_grad = (out_grad.astype(jnp.float32) + norm_back(summed_grad, centred, inv_scale, gain_vector)).astype(jnp.bfloat16)
    return (input_grad, normed, qkv_full, context_full)

def reference(inputs, cotangent, lengths, down_qkv, down_out, down_gain, up_qkv, up_out, up_gain):
    qkv_total = jnp.zeros((SECTIONS, D, 3, HD), jnp.float32)
    out_total = jnp.zeros((SECTIONS, D, HD), jnp.float32)
    for replica in range(N_DP):
        low_row = replica * TOK
        for direction in range(2):
            allowed = doc_mask(lengths[direction, replica], TOK)
            if direction == 0:
                tables = (down_qkv, down_out, down_gain)
                section_order = [section_index for section_index in range(SECTIONS)]
            else:
                tables = (up_qkv, up_out, up_gain)
                section_order = [SECTIONS - 1 - section_index for section_index in range(SECTIONS)]
            section_input = inputs[direction, low_row:low_row + TOK]
            saved_inputs = []
            for section_index in range(SECTIONS):
                slot_index = section_order[section_index]
                saved_inputs.append(section_input)
                if section_index < SECTIONS - 1:
                    section_input = section_front(section_input, tables[2][slot_index].astype(jnp.float32), tables[0][slot_index], tables[1][slot_index], allowed)
            out_grad = cotangent[direction, low_row:low_row + TOK]
            for section_index in range(SECTIONS - 1, -1, -1):
                slot_index = section_order[section_index]
                input_grad, normed, qkv_full, context_full = section_back(saved_inputs[section_index], out_grad, tables[2][slot_index].astype(jnp.float32), tables[0][slot_index], tables[1][slot_index], allowed, section_index > 0)
                qkv_term = jnp.einsum('tc,tjh->cjh', normed.astype(jnp.float32), qkv_full.astype(jnp.float32))
                out_term = jnp.einsum('tc,th->ch', out_grad.astype(jnp.float32), context_full.astype(jnp.float32))
                qkv_total = qkv_total.at[section_index].add(qkv_term)
                out_total = out_total.at[section_index].add(out_term)
                out_grad = input_grad
    return (qkv_total / N_DP, out_total / N_DP)
```

```python
import functools
import jax
import jax.numpy as jnp
from jax import lax
from jax.experimental import pallas as pl
from jax.experimental.pallas import tpu as pltpu
from jax.sharding import PartitionSpec as P

HS = 128
EPS = 1e-05
FACTOR = HS ** (-0.5)
F32 = jnp.float32
BF16 = jnp.bfloat16
SHIFTS = (2, 1, 3, 0)
VMEM_LIMIT = 40 * 1024 * 1024


def dot_nn(a, b):
    return lax.dot_general(a, b, (((1,), (0,)), ((), ())), preferred_element_type=F32)


def dot_nt(a, b):
    return lax.dot_general(a, b, (((1,), (1,)), ((), ())), preferred_element_type=F32)


def dot_tn(a, b):
    return lax.dot_general(a, b, (((0,), (0,)), ((), ())), preferred_element_type=F32)


def piece_rows(z, i, half):
    return pl.multiple_of(64 * half + 16 * lax.rem(z + 4 - SHIFTS[i], 4), 16)


def start_weights(d, down, up, held, sems):
    for choice, refs in ((0, down), (1, up)):

        @pl.when(d == choice)
        def _():
            for n, (source, target) in enumerate(zip(refs, held)):
                pltpu.make_async_copy(source, target, sems.at[n]).start()


def wait_weights(n, source, target, sems):
    pltpu.make_async_copy(source, target, sems.at[n]).wait()


def front_kernel(
    last, sc, own, oth, gain, allowed, wd, wu, od, ou, xn_i, qkv_i, prob_i, ctx_i, *refs
):
    if last:
        xn_o, qkv_o, prob_o, ctx_o, w, o, xn, qkv, prob, ctx, wsem, ssem = refs
    else:
        keep, send, xn_o, qkv_o, prob_o, ctx_o, w, o, xn, qkv, prob, ctx, wsem, ssem = refs
    active, d, c, z = sc[0], sc[1], sc[2], sc[3]

    @pl.when(active == 1)
    def _():
        held = [w.at[0], w.at[1], w.at[2]] + ([] if last else [o])
        down = [wd.at[0], wd.at[1], wd.at[2]] + ([] if last else [od])
        up = [wu.at[0], wu.at[1], wu.at[2]] + ([] if last else [ou])
        start_weights(d, down, up, held, wsem)
        g = gain[pl.ds(d, 1), :]
        for ref, half in ((own, c), (oth, 1 - c)):
            for i in range(4):
                x = ref[16 * i : 16 * i + 16, :].astype(F32)
                xc = x - jnp.mean(x, axis=-1, keepdims=True)
                rstd = lax.rsqrt(jnp.mean(xc * xc, axis=-1, keepdims=True) + EPS)
                xn[pl.ds(piece_rows(z, i, half), 16), :] = (xc * rstd * g).astype(BF16)
        copies = [pltpu.make_async_copy(xn, xn_o.at[d], ssem.at[0])]
        copies[0].start()
        for j in range(3):
            wait_weights(j, down[j], held[j], wsem)
            qkv[j] = dot_nn(xn[...], w[j]).astype(BF16)
        copies.append(pltpu.make_async_copy(qkv, qkv_o.at[d], ssem.at[1]))
        copies[1].start()
        mask = allowed[d] > 0.5
        for h in range(3):
            cols = slice(h * HS, h * HS + HS)
            s = dot_nt(qkv[0, :, cols], qkv[1, :, cols]) * FACTOR
            s = jnp.where(mask, s, -1e30)
            e = jnp.exp(s - jnp.max(s, axis=-1, keepdims=True))
            p = e / jnp.sum(e, axis=-1, keepdims=True)
            prob[h] = p
            ctx[:, cols] = dot_nn(p.astype(BF16), qkv[2, :, cols]).astype(BF16)
        copies.append(pltpu.make_async_copy(prob, prob_o.at[d], ssem.at[2]))
        copies.append(pltpu.make_async_copy(ctx, ctx_o.at[d], ssem.at[3]))
        copies[2].start()
        copies[3].start()
        if not last:
            lhs = jnp.concatenate(
                [
                    ctx[pl.ds(pl.multiple_of(64 * (1 - c), 64), 64), :],
                    ctx[pl.ds(pl.multiple_of(64 * c, 64), 64), :],
                ],
                axis=0,
            )
            wait_weights(3, od, o, wsem)
            for n in range(5):
                cols = slice(512 * n, 512 * n + 512)
                part = dot_nt(lhs, o[cols, :]).astype(BF16)
                send[:, cols] = part[:64]
                keep[:, cols] = part[64:]
        for copy in copies:
            copy.wait()


def back_kernel(last, sc, own, oth, wd, wu, od, ou, qkv_i, prob_i, dy_i, dqkv_i, *refs):
    if last:
        dy_o, dqkv_o, w, o, dy, qkv, prob, dqkv, wsem, ssem = refs
    else:
        keep, send, dy_o, dqkv_o, w, o, dy, qkv, prob, dqkv, wsem, ssem = refs
    active, d, c, z = sc[0], sc[1], sc[2], sc[3]

    @pl.when(active == 1)
    def _():
        held = [o] + ([] if last else [w.at[0], w.at[1], w.at[2]])
        down = [od] + ([] if last else [wd.at[0], wd.at[1], wd.at[2]])
        up = [ou] + ([] if last else [wu.at[0], wu.at[1], wu.at[2]])
        loads = [
            pltpu.make_async_copy(qkv_i.at[d], qkv, ssem.at[0]),
            pltpu.make_async_copy(prob_i.at[d], prob, ssem.at[1]),
        ]
        start_weights(d, down[:1], up[:1], held[:1], wsem)
        for load in loads:
            load.start()
        if not last:
            for choice, refs_ in ((0, down), (1, up)):

                @pl.when(d == choice)
                def _():
                    for n in range(1, 4):
                        pltpu.make_async_copy(refs_[n], held[n], wsem.at[n]).start()

        for ref, half in ((own, c), (oth, 1 - c)):
            for i in range(4):
                dy[pl.ds(piece_rows(z, i, half), 16), :] = ref[16 * i : 16 * i + 16, :]
        copies = [pltpu.make_async_copy(dy, dy_o.at[d], ssem.at[2])]
        copies[0].start()
        wait_weights(0, od, o, wsem)
        dctx = dot_nn(dy[...], o[...]).astype(BF16)
        for load in loads:
            load.wait()
        for h in range(3):
            cols = slice(h * HS, h * HS + HS)
            p = prob[h]
            dctx_h = dctx[:, cols]
            dp = dot_nt(dctx_h, qkv[2, :, cols])
            inner = jnp.sum(p * dp, axis=-1, keepdims=True)
            ds = (p * (dp - inner) * FACTOR).astype(BF16)
            dqkv[0, :, cols] = dot_nn(ds, qkv[1, :, cols]).astype(BF16)
            dqkv[1, :, cols] = dot_tn(ds, qkv[0, :, cols]).astype(BF16)
            dqkv[2, :, cols] = dot_tn(p.astype(BF16), dctx_h).astype(BF16)
        copies.append(pltpu.make_async_copy(dqkv, dqkv_o.at[d], ssem.at[3]))
        copies[1].start()
        if not last:
            lhs = []
            for j in range(3):
                lhs.append(
                    jnp.concatenate(
                        [
                            dqkv[j, pl.ds(pl.multiple_of(64 * (1 - c), 64), 64), :],
                            dqkv[j, pl.ds(pl.multiple_of(64 * c, 64), 64), :],
                        ],
                        axis=0,
                    )
                )
            for j in range(3):
                wait_weights(1 + j, wd.at[j], w.at[j], wsem)
            for n in range(5):
                cols = slice(512 * n, 512 * n + 512)
                part = dot_nt(lhs[0], w[0, cols, :])
                part += dot_nt(lhs[1], w[1, cols, :])
                part += dot_nt(lhs[2], w[2, cols, :])
                part = part.astype(BF16)
                send[:, cols] = part[:64]
                keep[:, cols] = part[64:]
        for copy in copies:
            copy.wait()


ANY = pl.BlockSpec(memory_space=pl.ANY)
VM = pl.BlockSpec(memory_space=pltpu.VMEM)
SM = pl.BlockSpec(memory_space=pltpu.SMEM)


def like(a):
    return jax.ShapeDtypeStruct(a.shape, a.dtype)


def spread_like(rows, width):
    return jax.ShapeDtypeStruct((rows, width), BF16)


def front_call(last, sc, own, oth, gain, allowed, weights, state):
    rows, width = own.shape
    wide = weights[2].shape[1]
    xn, qkv, prob, ctx = state
    halves = [] if last else [spread_like(rows, width)] * 2
    first = len(halves)
    return pl.pallas_call(
        functools.partial(front_kernel, last),
        out_shape=halves + [like(a) for a in state],
        in_specs=[SM, VM, VM, VM, VM] + [ANY] * 8,
        out_specs=[VM] * first + [ANY] * 4,
        input_output_aliases={9 + n: first + n for n in range(4)},
        scratch_shapes=[
            pltpu.VMEM((3, width, wide), BF16),
            pltpu.VMEM((width, wide), BF16),
            pltpu.VMEM(xn.shape[1:], BF16),
            pltpu.VMEM(qkv.shape[1:], BF16),
            pltpu.VMEM(prob.shape[1:], F32),
            pltpu.VMEM(ctx.shape[1:], BF16),
            pltpu.SemaphoreType.DMA((4,)),
            pltpu.SemaphoreType.DMA((4,)),
        ],
        compiler_params=pltpu.CompilerParams(vmem_limit_bytes=VMEM_LIMIT),
        cost_estimate=pl.CostEstimate(
            flops=2 * 128 * width * wide * 4, bytes_accessed=8 * width * wide, transcendentals=0
        ),
        name="front",
    )(sc, own, oth, gain, allowed, *weights, *state)


def back_call(last, sc, own, oth, weights, qkv, prob, dy, dqkv):
    rows, width = own.shape
    wide = weights[2].shape[1]
    halves = [] if last else [spread_like(rows, width)] * 2
    first = len(halves)
    return pl.pallas_call(
        functools.partial(back_kernel, last),
        out_shape=halves + [like(dy), like(dqkv)],
        in_specs=[SM, VM, VM] + [ANY] * 8,
        out_specs=[VM] * first + [ANY] * 2,
        input_output_aliases={9: first, 10: first + 1},
        scratch_shapes=[
            pltpu.VMEM((3, width, wide), BF16),
            pltpu.VMEM((width, wide), BF16),
            pltpu.VMEM(dy.shape[1:], BF16),
            pltpu.VMEM(qkv.shape[1:], BF16),
            pltpu.VMEM(prob.shape[1:], F32),
            pltpu.VMEM(dqkv.shape[1:], BF16),
            pltpu.SemaphoreType.DMA((4,)),
            pltpu.SemaphoreType.DMA((4,)),
        ],
        compiler_params=pltpu.CompilerParams(vmem_limit_bytes=VMEM_LIMIT),
        cost_estimate=pl.CostEstimate(
            flops=2 * 128 * width * wide * 4, bytes_accessed=8 * width * wide, transcendentals=0
        ),
        name="back",
    )(sc, own, oth, *weights, qkv, prob, dy, dqkv)


def alloc_kernel(*refs):
    pass


def alloc(shapes):
    return pl.pallas_call(
        alloc_kernel,
        out_shape=[jax.ShapeDtypeStruct(s, t) for s, t in shapes],
        out_specs=[ANY] * len(shapes),
        name="alloc",
    )()


def stage_partner(t, p):
    if t % 2 == 0:
        return p ^ 1
    if t == 3:
        return (7, 2, 1, 4, 3, 6, 5, 0)[p]
    return (3, 2, 1, 0, 7, 6, 5, 4)[p]


AXES = ("pipe", "tensor")


def permute(x, target):
    pairs = []
    for p in range(8):
        for z in range(4):
            for c in range(2):
                tp, tz, tc = target(p, z, c)
                pairs.append((p * 8 + z * 2 + c, tp * 8 + tz * 2 + tc))
    return lax.ppermute(x, AXES, pairs)


def other_core(x):
    return permute(x, lambda p, z, c: (p, z, 1 - c))


def sum_over_tensor(keep, send, z):
    pair = (keep.astype(F32) + other_core(send).astype(F32)).astype(BF16)
    parts = []
    for k in (2, 1, 3):
        block = lax.dynamic_slice_in_dim(pair, 16 * lax.rem(z + k, 4), 16, 0)
        parts.append(permute(block, lambda p, zz, c: (p, (zz + k) % 4, c)))
    own = lax.dynamic_slice_in_dim(pair, 16 * z, 16, 0)
    return own.astype(F32) + parts[0].astype(F32) + parts[1].astype(F32) + parts[2].astype(F32)


def hop_and_spread(block, t):
    pieces = [
        permute(block, lambda p, z, c: (stage_partner(t, p), (z + k) % 4, c)) for k in SHIFTS
    ]
    own = jnp.concatenate(pieces, axis=0)
    return own, other_core(own), pieces[3]


def doc_mask(doc_lengths, row_count):
    doc_ends = jnp.cumsum(doc_lengths)
    places = jnp.arange(row_count, dtype=jnp.int32)
    segment = jnp.sum((places[:, None] >= doc_ends[None, :]).astype(jnp.int32), axis=1)
    return (segment[:, None] == segment[None, :]) & (places[None, :] <= places[:, None])


def in_pieces(x, z, c):
    halves = []
    for half in (c, 1 - c):
        halves.append(
            jnp.concatenate(
                [
                    lax.dynamic_slice_in_dim(x, 64 * half + 16 * lax.rem(z + 4 - k, 4), 16, 0)
                    for k in SHIFTS
                ],
                axis=0,
            )
        )
    return halves[0], halves[1], halves[0][48:]


def mean(x):
    return jnp.mean(x, axis=-1, keepdims=True)


def local(inputs, cotangent, lengths, down_qkv, down_out, down_gain, up_qkv, up_out, up_gain):
    place = lax.axis_index("pipe")
    tensor = lax.axis_index("tensor")
    z, c = tensor // 2, tensor % 2
    rows, width = inputs.shape[1], inputs.shape[2]
    wide = down_out.shape[2]
    weights = (
        jnp.transpose(down_qkv[0], (1, 0, 2)),
        jnp.transpose(up_qkv[0], (1, 0, 2)),
        down_out[0],
        up_out[0],
    )
    gain = jnp.concatenate([down_gain, up_gain], axis=0).astype(F32)
    allowed = jnp.stack([doc_mask(lengths[r, 0], rows) for r in range(2)]).astype(F32)

    def scalars(is_down, is_up):
        active = (is_down | is_up).astype(jnp.int32)
        return jnp.stack([active, is_up.astype(jnp.int32), c, z]).astype(jnp.int32)

    state = alloc(
        [
            ((2, rows, width), BF16),
            ((2, 3, rows, wide), BF16),
            ((2, 3, rows, rows), F32),
            ((2, rows, wide), BF16),
        ]
    )
    dy_state, dqkv_state = alloc([((2, rows, width), BF16), ((2, 3, rows, wide), BF16)])

    own, oth, block = in_pieces(jnp.where(place == 0, inputs[0], inputs[1]), z, c)
    kept = [block, block]
    for t in range(8):
        is_down, is_up = place == t, place == 7 - t
        sc = scalars(is_down, is_up)
        kept = [jnp.where(is_down, block, kept[0]), jnp.where(is_up, block, kept[1])]
        if t < 7:
            keep, send, *state = front_call(False, sc, own, oth, gain, allowed, weights, state)
            total = sum_over_tensor(keep, send, z)
            result = (block.astype(F32) + total).astype(BF16)
            own, oth, block = hop_and_spread(result, t)
        else:
            state = front_call(True, sc, own, oth, gain, allowed, weights, state)
    xn, qkv, prob, ctx = state

    x = jnp.stack(kept).astype(F32)
    xc = x - mean(x)
    rstd = lax.rsqrt(mean(xc * xc) + EPS)
    xhat = xc * rstd

    own, oth, block = in_pieces(jnp.where(place == 7, cotangent[0], cotangent[1]), z, c)
    for t in range(8):
        is_down, is_up = place == 7 - t, place == t
        sc = scalars(is_down, is_up)
        if t < 7:
            keep, send, dy_state, dqkv_state = back_call(
                False, sc, own, oth, weights, qkv, prob, dy_state, dqkv_state
            )
            dxn = sum_over_tensor(keep, send, z)
            xhat_d = jnp.where(is_down, xhat[0], xhat[1])
            rstd_d = jnp.where(is_down, rstd[0], rstd[1])
            gr = dxn * jnp.where(is_down, gain[0:1], gain[1:2])
            change = rstd_d * (gr - mean(gr) - xhat_d * mean(gr * xhat_d))
            result = (block.astype(F32) + change).astype(BF16)
            own, oth, block = hop_and_spread(result, t)
        else:
            dy_state, dqkv_state = back_call(
                True, sc, own, oth, weights, qkv, prob, dy_state, dqkv_state
            )

    b = lax.axis_index("dp")
    half = width // 2

    def feature_half(a, which):
        return lax.dynamic_slice_in_dim(a, which * half, half, axis=-1)

    def pack(d, which):
        return jnp.concatenate(
            [
                feature_half(xn[d], which),
                feature_half(dy_state[d], which),
                ctx[d],
                dqkv_state[d, 0],
                dqkv_state[d, 1],
                dqkv_state[d, 2],
            ],
            axis=1,
        )

    def mirror(a, flip):
        pairs = [(p * 2 + bb, (7 - p) * 2 + (bb ^ flip)) for bb in range(2) for p in range(8)]
        return lax.ppermute(a, ("pipe", "dp"), pairs)

    packs = [
        pack(0, b),
        lax.ppermute(pack(0, 1 - b), "dp", [(0, 1), (1, 0)]),
        mirror(pack(1, b), 0),
        mirror(pack(1, 1 - b), 1),
    ]
    every = jnp.concatenate(packs, axis=0)
    xn_all = every[:, :half]
    dy_all = every[:, half : 2 * half]
    ctx_all = every[:, 2 * half : 2 * half + wide]
    dqkv_all = every[:, 2 * half + wide :]
    grad_qkv = dot_tn(xn_all, dqkv_all) * 0.5
    grad_out = dot_tn(dy_all, ctx_all) * 0.5
    return grad_qkv.reshape(1, half, 3, wide), grad_out.reshape(1, half, wide)


def solution(mesh):
    placed = (
        P(None, "dp", None),
        P(None, "dp", None),
        P(None, "dp", None),
        P("pipe", None, None, "tensor"),
        P("pipe", None, "tensor"),
        P("pipe", None),
        P("pipe", None, None, "tensor"),
        P("pipe", None, "tensor"),
        P("pipe", None),
    )
    return jax.shard_map(
        local,
        mesh=mesh,
        in_specs=placed,
        out_specs=(P("pipe", "dp", None, "tensor"), P("pipe", "dp", "tensor")),
        check_vma=False,
    )
```

```python
import functools
import jax
import jax.numpy as jnp
from jax import lax
from jax.experimental import pallas as pl
from jax.experimental.pallas import tpu as pltpu
from jax.sharding import PartitionSpec as P

HS = 128
EPS = 1e-05
FACTOR = HS ** (-0.5)
F32 = jnp.float32
BF16 = jnp.bfloat16
SHIFTS = (0, 1, 3, 2)
WEIGHT_PARTS = 2
VMEM_LIMIT = 52 * 1024 * 1024


def dot_nn(a, b):
    return lax.dot_general(a, b, (((1,), (0,)), ((), ())), preferred_element_type=F32)


def dot_nt(a, b):
    return lax.dot_general(a, b, (((1,), (1,)), ((), ())), preferred_element_type=F32)


def dot_tn(a, b):
    return lax.dot_general(a, b, (((0,), (0,)), ((), ())), preferred_element_type=F32)


def piece_rows(z, i, half):
    return pl.multiple_of(64 * half + 16 * lax.rem(z + 4 - SHIFTS[i], 4), 16)


def start_weights(d, down, up, held, sems):
    for choice, refs in ((0, down), (1, up)):

        @pl.when(d == choice)
        def _():
            for n, (source, target) in enumerate(zip(refs, held)):
                size = source.shape[0] // WEIGHT_PARTS
                for m in range(WEIGHT_PARTS):
                    part = pl.ds(m * size, size)
                    pltpu.make_async_copy(source.at[part], target.at[part], sems.at[n]).start()


def wait_weights(n, source, target, sems):
    pltpu.make_async_copy(source, target, sems.at[n]).wait()


def front_kernel(
    last, sc, own, oth, gain, allowed, wd, wu, od, ou, xn_i, qkv_i, prob_i, ctx_i, *refs
):
    if last:
        xn_o, qkv_o, prob_o, ctx_o, w, o, xn, qkv, prob, ctx, wsem, ssem = refs
    else:
        keep, send, xn_o, qkv_o, prob_o, ctx_o, w, o, xn, qkv, prob, ctx, wsem, ssem = refs
    active, d, c, z = sc[0], sc[1], sc[2], sc[3]

    @pl.when(active == 1)
    def _():
        held = [w.at[0], w.at[1], w.at[2]] + ([] if last else [o])
        down = [wd.at[0], wd.at[1], wd.at[2]] + ([] if last else [od])
        up = [wu.at[0], wu.at[1], wu.at[2]] + ([] if last else [ou])
        start_weights(d, down, up, held, wsem)
        g = gain[pl.ds(d, 1), :]
        for ref, half in ((own, c), (oth, 1 - c)):
            for i in range(4):
                x = ref[16 * i : 16 * i + 16, :].astype(F32)
                xc = x - jnp.mean(x, axis=-1, keepdims=True)
                rstd = lax.rsqrt(jnp.mean(xc * xc, axis=-1, keepdims=True) + EPS)
                xn[pl.ds(piece_rows(z, i, half), 16), :] = (xc * rstd * g).astype(BF16)
        copies = [pltpu.make_async_copy(xn, xn_o.at[d], ssem.at[0])]
        copies[0].start()
        for j in range(3):
            wait_weights(j, down[j], held[j], wsem)
            qkv[j] = dot_nn(xn[...], w[j]).astype(BF16)
        copies.append(pltpu.make_async_copy(qkv, qkv_o.at[d], ssem.at[1]))
        copies[1].start()
        mask = allowed[d] > 0.5
        for h in range(3):
            cols = slice(h * HS, h * HS + HS)
            s = dot_nt(qkv[0, :, cols], qkv[1, :, cols]) * FACTOR
            s = jnp.where(mask, s, -1e30)
            e = jnp.exp(s - jnp.max(s, axis=-1, keepdims=True))
            p = e / jnp.sum(e, axis=-1, keepdims=True)
            prob[h] = p
            ctx_h = dot_nn(p.astype(BF16), qkv[2, :, cols]).astype(BF16)
            for side in range(2):
                at = side * 3 * HS + h * HS
                ctx[:, at : at + HS] = ctx_h[64 * side : 64 * side + 64]
        copies.append(pltpu.make_async_copy(prob, prob_o.at[d], ssem.at[2]))
        copies.append(pltpu.make_async_copy(ctx, ctx_o.at[d], ssem.at[3]))
        copies[2].start()
        copies[3].start()
        if not last:
            lhs = jnp.concatenate(
                [
                    ctx[:, pl.ds(pl.multiple_of(side * 3 * HS, HS), 3 * HS)]
                    for side in (1 - c, c)
                ],
                axis=0,
            )
            wait_weights(3, od, o, wsem)
            for n in range(5):
                cols = slice(512 * n, 512 * n + 512)
                part = dot_nt(lhs, o[cols, :]).astype(BF16)
                send[:, cols] = part[:64]
                keep[:, cols] = part[64:]
        for copy in copies:
            copy.wait()


def back_kernel(last, sc, own, oth, wd, wu, od, ou, qkv_i, prob_i, dy_i, dqkv_i, *refs):
    if last:
        dy_o, dqkv_o, w, o, dy, qkv, prob, dqkv, wsem, ssem = refs
    else:
        keep, send, dy_o, dqkv_o, w, o, dy, qkv, prob, dqkv, wsem, ssem = refs
    active, d, c, z = sc[0], sc[1], sc[2], sc[3]

    @pl.when(active == 1)
    def _():
        held = [o] + ([] if last else [w.at[0], w.at[1], w.at[2]])
        down = [od] + ([] if last else [wd.at[0], wd.at[1], wd.at[2]])
        up = [ou] + ([] if last else [wu.at[0], wu.at[1], wu.at[2]])
        loads = [
            pltpu.make_async_copy(qkv_i.at[d], qkv, ssem.at[0]),
            pltpu.make_async_copy(prob_i.at[d], prob, ssem.at[1]),
        ]
        start_weights(d, down, up, held, wsem)
        for load in loads:
            load.start()
        for ref, half in ((own, c), (oth, 1 - c)):
            for i in range(4):
                dy[pl.ds(piece_rows(z, i, half), 16), :] = ref[16 * i : 16 * i + 16, :]
        copies = [pltpu.make_async_copy(dy, dy_o.at[d], ssem.at[2])]
        copies[0].start()
        wait_weights(0, od, o, wsem)
        dctx = dot_nn(dy[...], o[...]).astype(BF16)
        for load in loads:
            load.wait()
        for h in range(3):
            cols = slice(h * HS, h * HS + HS)
            p = prob[h]
            dctx_h = dctx[:, cols]
            dp = dot_nt(dctx_h, qkv[2, :, cols])
            inner = jnp.sum(p * dp, axis=-1, keepdims=True)
            ds = (p * (dp - inner) * FACTOR).astype(BF16)
            grads = (
                dot_nn(ds, qkv[1, :, cols]).astype(BF16),
                dot_tn(ds, qkv[0, :, cols]).astype(BF16),
                dot_tn(p.astype(BF16), dctx_h).astype(BF16),
            )
            for j in range(3):
                for side in range(2):
                    at = (side * 3 + j) * 3 * HS + h * HS
                    dqkv[:, at : at + HS] = grads[j][64 * side : 64 * side + 64]
        copies.append(pltpu.make_async_copy(dqkv, dqkv_o.at[d], ssem.at[3]))
        copies[1].start()
        if not last:
            lhs = []
            for j in range(3):
                lhs.append(
                    jnp.concatenate(
                        [
                            dqkv[:, pl.ds(pl.multiple_of((side * 3 + j) * 3 * HS, HS), 3 * HS)]
                            for side in (1 - c, c)
                        ],
                        axis=0,
                    )
                )
            for j in range(3):
                wait_weights(1 + j, wd.at[j], w.at[j], wsem)
            for n in range(5):
                cols = slice(512 * n, 512 * n + 512)
                part = dot_nt(lhs[0], w[0, cols, :])
                part += dot_nt(lhs[1], w[1, cols, :])
                part += dot_nt(lhs[2], w[2, cols, :])
                part = part.astype(BF16)
                send[:, cols] = part[:64]
                keep[:, cols] = part[64:]
        for copy in copies:
            copy.wait()


ANY = pl.BlockSpec(memory_space=pltpu.HBM)
VM = pl.BlockSpec(memory_space=pltpu.VMEM)
SM = pl.BlockSpec(memory_space=pltpu.SMEM)


def like(a):
    return jax.ShapeDtypeStruct(a.shape, a.dtype)


def spread_like(rows, width):
    return jax.ShapeDtypeStruct((rows, width), BF16)


def front_call(last, sc, own, oth, gain, allowed, weights, state):
    rows, width = own.shape
    wide = weights[2].shape[1]
    xn, qkv, prob, ctx = state
    halves = [] if last else [spread_like(rows, width)] * 2
    first = len(halves)
    return pl.pallas_call(
        functools.partial(front_kernel, last),
        out_shape=halves + [like(a) for a in state],
        in_specs=[SM, VM, VM, VM, VM] + [ANY] * 8,
        out_specs=[VM] * first + [ANY] * 4,
        input_output_aliases={9 + n: first + n for n in range(4)},
        scratch_shapes=[
            pltpu.VMEM((3, width, wide), BF16),
            pltpu.VMEM((width, wide), BF16),
            pltpu.VMEM(xn.shape[1:], BF16),
            pltpu.VMEM(qkv.shape[1:], BF16),
            pltpu.VMEM(prob.shape[1:], F32),
            pltpu.VMEM(ctx.shape[1:], BF16),
            pltpu.SemaphoreType.DMA((4,)),
            pltpu.SemaphoreType.DMA((4,)),
        ],
        compiler_params=pltpu.CompilerParams(vmem_limit_bytes=VMEM_LIMIT),
        cost_estimate=pl.CostEstimate(
            flops=2 * 128 * width * wide * 4, bytes_accessed=8 * width * wide, transcendentals=0
        ),
        name="front",
    )(sc, own, oth, gain, allowed, *weights, *state)


def back_call(last, sc, own, oth, weights, qkv, prob, dy, dqkv):
    rows, width = own.shape
    wide = weights[2].shape[1]
    halves = [] if last else [spread_like(rows, width)] * 2
    first = len(halves)
    return pl.pallas_call(
        functools.partial(back_kernel, last),
        out_shape=halves + [like(dy), like(dqkv)],
        in_specs=[SM, VM, VM] + [ANY] * 8,
        out_specs=[VM] * first + [ANY] * 2,
        input_output_aliases={9: first, 10: first + 1},
        scratch_shapes=[
            pltpu.VMEM((3, width, wide), BF16),
            pltpu.VMEM((width, wide), BF16),
            pltpu.VMEM(dy.shape[1:], BF16),
            pltpu.VMEM(qkv.shape[1:], BF16),
            pltpu.VMEM(prob.shape[1:], F32),
            pltpu.VMEM(dqkv.shape[1:], BF16),
            pltpu.SemaphoreType.DMA((4,)),
            pltpu.SemaphoreType.DMA((4,)),
        ],
        compiler_params=pltpu.CompilerParams(vmem_limit_bytes=VMEM_LIMIT),
        cost_estimate=pl.CostEstimate(
            flops=2 * 128 * width * wide * 4, bytes_accessed=8 * width * wide, transcendentals=0
        ),
        name="back",
    )(sc, own, oth, *weights, qkv, prob, dy, dqkv)


def alloc_kernel(*refs):
    pass


def alloc(shapes):
    return pl.pallas_call(
        alloc_kernel,
        out_shape=[jax.ShapeDtypeStruct(s, t) for s, t in shapes],
        out_specs=[ANY] * len(shapes),
        name="alloc",
    )()


def stage_partner(t, p):
    if t % 2 == 0:
        return p ^ 1
    if t == 3:
        return (7, 2, 1, 4, 3, 6, 5, 0)[p]
    return (3, 2, 1, 0, 7, 6, 5, 4)[p]


AXES = ("pipe", "tensor")


def permute(x, target):
    pairs = []
    for p in range(8):
        for z in range(4):
            for c in range(2):
                tp, tz, tc = target(p, z, c)
                pairs.append((p * 8 + z * 2 + c, tp * 8 + tz * 2 + tc))
    return lax.ppermute(x, AXES, pairs)


def other_core(x):
    return permute(x, lambda p, z, c: (p, z, 1 - c))


def sum_over_tensor(keep, send, z):
    pair = (keep.astype(F32) + other_core(send).astype(F32)).astype(BF16)
    parts = []
    for k in (2, 1, 3):
        block = lax.dynamic_slice_in_dim(pair, 16 * lax.rem(z + k, 4), 16, 0)
        parts.append(permute(block, lambda p, zz, c: (p, (zz + k) % 4, c)))
    own = lax.dynamic_slice_in_dim(pair, 16 * z, 16, 0)
    return own.astype(F32) + parts[0].astype(F32) + parts[1].astype(F32) + parts[2].astype(F32)


def hop_and_spread(block, t):
    pieces = [
        permute(block, lambda p, z, c: (stage_partner(t, p), (z + k) % 4, c)) for k in SHIFTS
    ]
    own = jnp.concatenate(pieces, axis=0)
    return own, other_core(own), pieces[0]


def mirror(a, flip):
    pairs = [(p * 2 + b, (7 - p) * 2 + (b ^ flip)) for b in range(2) for p in range(8)]
    return lax.ppermute(a, ("pipe", "dp"), pairs)


def swap_dp(a):
    return lax.ppermute(a, "dp", [(0, 1), (1, 0)])


def gather_items(pick, b):
    return [
        pick(0, b),
        swap_dp(pick(0, 1 - b)),
        mirror(pick(1, b), 0),
        mirror(pick(1, 1 - b), 1),
    ]


def grad_kernel(sc, *refs):
    xn_ctx, xn_oth, dy, dy_oth, dqkv = refs[0:4], refs[4], refs[5:9], refs[9], refs[10:14]
    grad_qkv, grad_out = refs[14:]
    step, wide = grad_out.shape
    half = xn_oth.shape[1]
    c = sc[2]
    rows = pl.ds(pl.multiple_of(pl.program_id(0) * step, step), step)

    def left(items, others):
        return jnp.concatenate([r[:, rows] for r in items] + [others[:, rows]], axis=0)

    def right(items, base, count, j):
        starts = [base + side * count * wide + j * wide for side in (c, 1 - c)]
        return jnp.concatenate(
            [r[:, pl.ds(pl.multiple_of(start, 128), wide)] for start in starts for r in items],
            axis=0,
        )

    lhs = left(xn_ctx, xn_oth)
    for j in range(3):
        grad_qkv[j] = dot_tn(lhs, right(dqkv, 0, 3, j)) * 0.5
    grad_out[...] = dot_tn(left(dy, dy_oth), right(xn_ctx, half, 1, 0)) * 0.5


def grad_call(sc, xn_ctx, xn_oth, dy, dy_oth, dqkv, wide):
    half = xn_oth.shape[1]
    step = 256
    items = (*xn_ctx, xn_oth, *dy, dy_oth, *dqkv)
    return pl.pallas_call(
        grad_kernel,
        grid=(half // step,),
        out_shape=[
            jax.ShapeDtypeStruct((3, half, wide), F32),
            jax.ShapeDtypeStruct((half, wide), F32),
        ],
        in_specs=[SM] + [pl.BlockSpec(a.shape, lambda i: (0, 0)) for a in items],
        out_specs=[
            pl.BlockSpec((3, step, wide), lambda i: (0, i, 0)),
            pl.BlockSpec((step, wide), lambda i: (i, 0)),
        ],
        compiler_params=pltpu.CompilerParams(vmem_limit_bytes=VMEM_LIMIT),
        name="grad",
    )(sc, *items)


def doc_mask(doc_lengths, row_count):
    doc_ends = jnp.cumsum(doc_lengths)
    places = jnp.arange(row_count, dtype=jnp.int32)
    segment = jnp.sum((places[:, None] >= doc_ends[None, :]).astype(jnp.int32), axis=1)
    return (segment[:, None] == segment[None, :]) & (places[None, :] <= places[:, None])


def in_pieces(x, z, c):
    halves = []
    for half in (c, 1 - c):
        halves.append(
            jnp.concatenate(
                [
                    lax.dynamic_slice_in_dim(x, 64 * half + 16 * lax.rem(z + 4 - k, 4), 16, 0)
                    for k in SHIFTS
                ],
                axis=0,
            )
        )
    return halves[0], halves[1], halves[0][:16]


def mean(x):
    return jnp.mean(x, axis=-1, keepdims=True)


def local(inputs, cotangent, lengths, down_qkv, down_out, down_gain, up_qkv, up_out, up_gain):
    place = lax.axis_index("pipe")
    tensor = lax.axis_index("tensor")
    z, c = tensor // 2, tensor % 2
    rows, width = inputs.shape[1], inputs.shape[2]
    wide = down_out.shape[2]
    weights = (
        jnp.transpose(down_qkv[0], (1, 0, 2)),
        jnp.transpose(up_qkv[0], (1, 0, 2)),
        down_out[0],
        up_out[0],
    )
    gain = jnp.concatenate([down_gain, up_gain], axis=0).astype(F32)
    allowed = jnp.stack([doc_mask(lengths[r, 0], rows) for r in range(2)]).astype(F32)

    def after(value, *others):
        return lax.optimization_barrier((value,) + others)[0]

    def scalars(is_down, is_up):
        active = (is_down | is_up).astype(jnp.int32)
        return jnp.stack([active, is_up.astype(jnp.int32), c, z]).astype(jnp.int32)

    state = alloc(
        [
            ((2, rows, width), BF16),
            ((2, 3, rows, wide), BF16),
            ((2, 3, rows, rows), F32),
            ((2, rows // 2, 2 * wide), BF16),
        ]
    )
    dy_state, dqkv_state = alloc([((2, rows, width), BF16), ((2, rows // 2, 6 * wide), BF16)])

    own, oth, block = in_pieces(jnp.where(place == 0, inputs[0], inputs[1]), z, c)
    kept = [block, block]
    for t in range(8):
        is_down, is_up = place == t, place == 7 - t
        sc = scalars(is_down, is_up)
        kept = [jnp.where(is_down, block, kept[0]), jnp.where(is_up, block, kept[1])]
        if t < 7:
            keep, send, *state = front_call(False, sc, own, oth, gain, allowed, weights, state)
            total = sum_over_tensor(keep, send, z)
            result = (block.astype(F32) + total).astype(BF16)
            own, oth, block = hop_and_spread(result, t)
        else:
            state = front_call(True, sc, own, oth, gain, allowed, weights, state)
    xn, qkv, prob, ctx = state
    b = lax.axis_index("dp")

    half = width // 2

    def features(a, which, core):
        return lax.dynamic_slice(a, (64 * core, which * half), (64, half))

    def other_halves(local_whole, items):
        received = other_core(jnp.concatenate([a[:, :half] for a in items[1:]], axis=0))
        return jnp.concatenate([features(local_whole, b, 1 - c), received], axis=0)

    xn_ctx = gather_items(
        lambda d, which: jnp.concatenate([features(xn[d], which, c), ctx[d]], axis=1), b
    )
    xn_oth = other_halves(xn[0], xn_ctx)

    x = jnp.stack(kept).astype(F32)
    xc = x - mean(x)
    rstd = lax.rsqrt(mean(xc * xc) + EPS)
    xhat = xc * rstd

    def tokens(own, oth):
        first, second = jnp.where(c == 0, own, oth), jnp.where(c == 0, oth, own)
        turned = jnp.concatenate([first, second], axis=0).reshape(2, 4, 16, width)
        order = [lax.rem(z + 4 - k, 4) for k in SHIFTS]
        blocks = [turned[:, 0]] * 4
        for place_to in range(4):
            for i in range(4):
                blocks[place_to] = jnp.where(order[i] == place_to, turned[:, i], blocks[place_to])
        return jnp.stack(blocks, axis=1).reshape(rows, width)

    own, oth, block = in_pieces(jnp.where(place == 7, cotangent[0], cotangent[1]), z, c)
    for t in range(8):
        is_down, is_up = place == 7 - t, place == t
        sc = scalars(is_down, is_up)
        if t < 7:
            keep, send, dy_state, dqkv_state = back_call(
                False, sc, own, oth, weights, qkv, prob, dy_state, dqkv_state
            )
            dxn = sum_over_tensor(keep, send, z)
            xhat_d = jnp.where(is_down, xhat[0], xhat[1])
            rstd_d = jnp.where(is_down, rstd[0], rstd[1])
            gr = dxn * jnp.where(is_down, gain[0:1], gain[1:2])
            change = rstd_d * (gr - mean(gr) - xhat_d * mean(gr * xhat_d))
            result = (block.astype(F32) + change).astype(BF16)
            own, oth, block = hop_and_spread(result, t)
            if t == 1:
                own, oth, block, xn_oth, *xn_ctx = lax.optimization_barrier(
                    (own, oth, block, xn_oth, *xn_ctx)
                )
        else:
            dy_now = [
                jnp.where(here, tokens(own, oth), dy_state[d])
                for d, here in enumerate((is_down, is_up))
            ]
            dy = gather_items(lambda d, which: features(dy_now[d], which, c), b)
            dy_oth = other_halves(dy_now[0], dy)
            dy_state, dqkv_state = back_call(
                True, sc, own, oth, weights, qkv, prob, dy_state, dqkv_state
            )

    dqkv = gather_items(lambda d, which: dqkv_state[d], b)
    grad_qkv, grad_out = grad_call(sc, xn_ctx, xn_oth, dy, dy_oth, dqkv, wide)
    return jnp.transpose(grad_qkv, (1, 0, 2))[None], grad_out[None]


def solution(mesh):
    placed = (
        P(None, "dp", None),
        P(None, "dp", None),
        P(None, "dp", None),
        P("pipe", None, None, "tensor"),
        P("pipe", None, "tensor"),
        P("pipe", None),
        P("pipe", None, None, "tensor"),
        P("pipe", None, "tensor"),
        P("pipe", None),
    )
    return jax.shard_map(
        local,
        mesh=mesh,
        in_specs=placed,
        out_specs=(P("pipe", "dp", None, "tensor"), P("pipe", "dp", "tensor")),
        check_vma=False,
    )
```

```python
import functools
import jax
import jax.numpy as jnp
from jax import lax
from jax.experimental import pallas as pl
from jax.experimental.pallas import tpu as pltpu
from jax.sharding import PartitionSpec as P

HS = 128
EPS = 1e-05
FACTOR = HS ** (-0.5)
F32 = jnp.float32
BF16 = jnp.bfloat16
SHIFTS = (0, 1, 3, 2)
WEIGHT_PARTS = 2
VMEM_LIMIT = 24 * 1024 * 1024


def dot_nn(a, b):
    return lax.dot_general(a, b, (((1,), (0,)), ((), ())), preferred_element_type=F32)


def dot_nt(a, b):
    return lax.dot_general(a, b, (((1,), (1,)), ((), ())), preferred_element_type=F32)


def dot_tn(a, b):
    return lax.dot_general(a, b, (((0,), (0,)), ((), ())), preferred_element_type=F32)


def piece_rows(z, i, half):
    return pl.multiple_of(64 * half + 16 * lax.rem(z + 4 - SHIFTS[i], 4), 16)


def start_weights(d, down, up, held, sems):
    for choice, refs in ((0, down), (1, up)):

        @pl.when(d == choice)
        def _():
            for n, (source, target) in enumerate(zip(refs, held)):
                size = source.shape[0] // WEIGHT_PARTS
                for m in range(WEIGHT_PARTS):
                    part = pl.ds(m * size, size)
                    pltpu.make_async_copy(source.at[part], target.at[part], sems.at[n]).start()


def wait_weights(n, source, target, sems):
    pltpu.make_async_copy(source, target, sems.at[n]).wait()


def front_kernel(
    last, sc, own, oth, gain, allowed, wd, wu, od, ou, xn_i, qkv_i, prob_i, ctx_i, *refs
):
    if last:
        xn_o, qkv_o, prob_o, ctx_o, w, o, xn, qkv, prob, ctx, wsem, ssem = refs
    else:
        keep, send, xn_o, qkv_o, prob_o, ctx_o, w, o, xn, qkv, prob, ctx, wsem, ssem = refs
    active, d, c, z = sc[0], sc[1], sc[2], sc[3]

    @pl.when(active == 1)
    def _():
        held = [w.at[0], w.at[1], w.at[2]] + ([] if last else [o])
        down = [wd.at[0], wd.at[1], wd.at[2]] + ([] if last else [od])
        up = [wu.at[0], wu.at[1], wu.at[2]] + ([] if last else [ou])
        start_weights(d, down, up, held, wsem)
        g = gain[pl.ds(d, 1), :]
        for ref, half in ((own, c), (oth, 1 - c)):
            for i in range(4):
                x = ref[16 * i : 16 * i + 16, :].astype(F32)
                xc = x - jnp.mean(x, axis=-1, keepdims=True)
                rstd = lax.rsqrt(jnp.mean(xc * xc, axis=-1, keepdims=True) + EPS)
                xn[pl.ds(piece_rows(z, i, half), 16), :] = (xc * rstd * g).astype(BF16)
        copies = [pltpu.make_async_copy(xn, xn_o.at[d], ssem.at[0])]
        copies[0].start()
        for j in range(3):
            wait_weights(j, down[j], held[j], wsem)
            qkv[j] = dot_nn(xn[...], w[j]).astype(BF16)
        copies.append(pltpu.make_async_copy(qkv, qkv_o.at[d], ssem.at[1]))
        copies[1].start()
        mask = allowed[d] > 0.5
        for h in range(3):
            cols = slice(h * HS, h * HS + HS)
            s = dot_nt(qkv[0, :, cols], qkv[1, :, cols]) * FACTOR
            s = jnp.where(mask, s, -1e30)
            e = jnp.exp(s - jnp.max(s, axis=-1, keepdims=True))
            p = e / jnp.sum(e, axis=-1, keepdims=True)
            prob[h] = p
            ctx_h = dot_nn(p.astype(BF16), qkv[2, :, cols]).astype(BF16)
            for side in range(2):
                at = side * 3 * HS + h * HS
                ctx[:, at : at + HS] = ctx_h[64 * side : 64 * side + 64]
        copies.append(pltpu.make_async_copy(prob, prob_o.at[d], ssem.at[2]))
        copies.append(pltpu.make_async_copy(ctx, ctx_o.at[d], ssem.at[3]))
        copies[2].start()
        copies[3].start()
        if not last:
            lhs = jnp.concatenate(
                [
                    ctx[:, pl.ds(pl.multiple_of(side * 3 * HS, HS), 3 * HS)]
                    for side in (1 - c, c)
                ],
                axis=0,
            )
            wait_weights(3, od, o, wsem)
            for n in range(5):
                cols = slice(512 * n, 512 * n + 512)
                part = dot_nt(lhs, o[cols, :]).astype(BF16)
                send[:, cols] = part[:64]
                keep[:, cols] = part[64:]
        for copy in copies:
            copy.wait()


def back_kernel(last, sc, own, oth, wd, wu, od, ou, qkv_i, prob_i, dy_i, dqkv_i, *refs):
    if last:
        dy_o, dqkv_o, w, o, dy, qkv, prob, dqkv, grads, wsem, ssem = refs
    else:
        keep, send, dy_o, dqkv_o, w, o, dy, qkv, prob, dqkv, grads, wsem, ssem = refs
    active, d, c, z = sc[0], sc[1], sc[2], sc[3]

    @pl.when(active == 1)
    def _():
        held = [o] + ([] if last else [w.at[0], w.at[1], w.at[2]])
        down = [od] + ([] if last else [wd.at[0], wd.at[1], wd.at[2]])
        up = [ou] + ([] if last else [wu.at[0], wu.at[1], wu.at[2]])
        loads = [
            pltpu.make_async_copy(qkv_i.at[d], qkv, ssem.at[0]),
            pltpu.make_async_copy(prob_i.at[d], prob, ssem.at[1]),
        ]
        start_weights(d, down, up, held, wsem)
        for load in loads:
            load.start()
        for ref, half in ((own, c), (oth, 1 - c)):
            for i in range(4):
                dy[pl.ds(piece_rows(z, i, half), 16), :] = ref[16 * i : 16 * i + 16, :]
        copies = [pltpu.make_async_copy(dy, dy_o.at[d], ssem.at[2])]
        copies[0].start()
        wait_weights(0, od, o, wsem)
        dctx = dot_nn(dy[...], o[...]).astype(BF16)
        for load in loads:
            load.wait()
        for h in range(3):
            cols = slice(h * HS, h * HS + HS)
            p = prob[h]
            dctx_h = dctx[:, cols]
            dp = dot_nt(dctx_h, qkv[2, :, cols])
            inner = jnp.sum(p * dp, axis=-1, keepdims=True)
            ds = (p * (dp - inner) * FACTOR).astype(BF16)
            grads[0, :, cols] = dot_nn(ds, qkv[1, :, cols]).astype(BF16)
            grads[1, :, cols] = dot_tn(ds, qkv[0, :, cols]).astype(BF16)
            grads[2, :, cols] = dot_tn(p.astype(BF16), dctx_h).astype(BF16)
        for j in range(3):
            for side in range(2):
                at = (side * 3 + j) * 3 * HS
                dqkv[:, at : at + 3 * HS] = grads[j, 64 * side : 64 * side + 64, :]
        copies.append(pltpu.make_async_copy(dqkv, dqkv_o.at[d], ssem.at[3]))
        copies[1].start()
        if not last:
            lhs = []
            for j in range(3):
                lhs.append(
                    jnp.concatenate(
                        [
                            grads[j, pl.ds(pl.multiple_of(64 * side, 64), 64), :]
                            for side in (1 - c, c)
                        ],
                        axis=0,
                    )
                )
            for j in range(3):
                wait_weights(1 + j, wd.at[j], w.at[j], wsem)
            for n in range(5):
                cols = slice(512 * n, 512 * n + 512)
                part = dot_nt(lhs[0], w[0, cols, :])
                part += dot_nt(lhs[1], w[1, cols, :])
                part += dot_nt(lhs[2], w[2, cols, :])
                part = part.astype(BF16)
                send[:, cols] = part[:64]
                keep[:, cols] = part[64:]
        for copy in copies:
            copy.wait()


ANY = pl.BlockSpec(memory_space=pltpu.HBM)
VM = pl.BlockSpec(memory_space=pltpu.VMEM)
SM = pl.BlockSpec(memory_space=pltpu.SMEM)


def like(a):
    return pltpu.HBM(a.shape, a.dtype)


def in_hbm(arrays):
    return [pltpu.with_memory_space_constraint(a, pltpu.HBM) for a in arrays]


def spread_like(rows, width):
    return jax.ShapeDtypeStruct((rows, width), BF16)


def front_call(last, sc, own, oth, gain, allowed, weights, state):
    rows, width = own.shape
    wide = weights[2].shape[1]
    xn, qkv, prob, ctx = state
    halves = [] if last else [spread_like(rows, width)] * 2
    first = len(halves)
    return pl.pallas_call(
        functools.partial(front_kernel, last),
        out_shape=halves + [like(a) for a in state],
        in_specs=[SM, VM, VM, VM, VM] + [ANY] * 8,
        out_specs=[VM] * first + [ANY] * 4,
        input_output_aliases={9 + n: first + n for n in range(4)},
        scratch_shapes=[
            pltpu.VMEM((3, width, wide), BF16),
            pltpu.VMEM((width, wide), BF16),
            pltpu.VMEM(xn.shape[1:], BF16),
            pltpu.VMEM(qkv.shape[1:], BF16),
            pltpu.VMEM(prob.shape[1:], F32),
            pltpu.VMEM(ctx.shape[1:], BF16),
            pltpu.SemaphoreType.DMA((4,)),
            pltpu.SemaphoreType.DMA((4,)),
        ],
        compiler_params=pltpu.CompilerParams(vmem_limit_bytes=VMEM_LIMIT),
        cost_estimate=pl.CostEstimate(
            flops=2 * 128 * width * wide * 4, bytes_accessed=8 * width * wide, transcendentals=0
        ),
        name="front",
    )(sc, own, oth, gain, allowed, *in_hbm((*weights, *state)))


def back_call(last, sc, own, oth, weights, qkv, prob, dy, dqkv):
    rows, width = own.shape
    wide = weights[2].shape[1]
    halves = [] if last else [spread_like(rows, width)] * 2
    first = len(halves)
    return pl.pallas_call(
        functools.partial(back_kernel, last),
        out_shape=halves + [like(dy), like(dqkv)],
        in_specs=[SM, VM, VM] + [ANY] * 8,
        out_specs=[VM] * first + [ANY] * 2,
        input_output_aliases={9: first, 10: first + 1},
        scratch_shapes=[
            pltpu.VMEM((3, width, wide), BF16),
            pltpu.VMEM((width, wide), BF16),
            pltpu.VMEM(dy.shape[1:], BF16),
            pltpu.VMEM(qkv.shape[1:], BF16),
            pltpu.VMEM(prob.shape[1:], F32),
            pltpu.VMEM(dqkv.shape[1:], BF16),
            pltpu.VMEM(qkv.shape[1:], BF16),
            pltpu.SemaphoreType.DMA((4,)),
            pltpu.SemaphoreType.DMA((4,)),
        ],
        compiler_params=pltpu.CompilerParams(vmem_limit_bytes=VMEM_LIMIT),
        cost_estimate=pl.CostEstimate(
            flops=2 * 128 * width * wide * 4, bytes_accessed=8 * width * wide, transcendentals=0
        ),
        name="back",
    )(sc, own, oth, *in_hbm((*weights, qkv, prob, dy, dqkv)))


def alloc_kernel(*refs):
    pass


def alloc(shapes):
    return pl.pallas_call(
        alloc_kernel,
        out_shape=[pltpu.HBM(s, t) for s, t in shapes],
        out_specs=[ANY] * len(shapes),
        name="alloc",
    )()


def stage_partner(t, p):
    if t % 2 == 0:
        return p ^ 1
    if t == 3:
        return (7, 2, 1, 4, 3, 6, 5, 0)[p]
    return (3, 2, 1, 0, 7, 6, 5, 4)[p]


AXES = ("pipe", "tensor")


def permute(x, target):
    pairs = []
    for p in range(8):
        for z in range(4):
            for c in range(2):
                tp, tz, tc = target(p, z, c)
                pairs.append((p * 8 + z * 2 + c, tp * 8 + tz * 2 + tc))
    return lax.ppermute(x, AXES, pairs)


def other_core(x):
    return permute(x, lambda p, z, c: (p, z, 1 - c))


def sum_over_tensor(keep, send, z):
    pair = (keep.astype(F32) + other_core(send).astype(F32)).astype(BF16)
    parts = []
    for k in (2, 1, 3):
        block = lax.dynamic_slice_in_dim(pair, 16 * lax.rem(z + k, 4), 16, 0)
        parts.append(permute(block, lambda p, zz, c: (p, (zz + k) % 4, c)))
    own = lax.dynamic_slice_in_dim(pair, 16 * z, 16, 0)
    return own.astype(F32) + parts[0].astype(F32) + parts[1].astype(F32) + parts[2].astype(F32)


def hop_and_spread(block, t):
    pieces = [
        permute(block, lambda p, z, c: (stage_partner(t, p), (z + k) % 4, c)) for k in SHIFTS
    ]
    own = jnp.concatenate(pieces, axis=0)
    return own, other_core(own), pieces[0]


def mirror(a, flip):
    pairs = [(p * 2 + b, (7 - p) * 2 + (b ^ flip)) for b in range(2) for p in range(8)]
    return lax.ppermute(a, ("pipe", "dp"), pairs)


def swap_dp(a):
    return lax.ppermute(a, "dp", [(0, 1), (1, 0)])


def gather_items(pick, b):
    return [
        pick(0, b),
        swap_dp(pick(0, 1 - b)),
        mirror(pick(1, b), 0),
        mirror(pick(1, 1 - b), 1),
    ]


def grad_kernel(sc, *refs):
    xn_ctx, xn_oth, dy, dy_oth, dqkv = refs[0:4], refs[4], refs[5:9], refs[9], refs[10:14]
    grad_qkv, grad_out = refs[14:]
    step, wide = grad_out.shape
    half = xn_oth.shape[1]
    c = sc[2]
    rows = pl.ds(pl.multiple_of(pl.program_id(0) * step, step), step)

    def left(items, others):
        return jnp.concatenate([r[:, rows] for r in items] + [others[:, rows]], axis=0)

    def right(items, base, count, j):
        starts = [base + side * count * wide + j * wide for side in (c, 1 - c)]
        return jnp.concatenate(
            [r[:, pl.ds(pl.multiple_of(start, 128), wide)] for start in starts for r in items],
            axis=0,
        )

    lhs = left(xn_ctx, xn_oth)
    for j in range(3):
        grad_qkv[j] = dot_tn(lhs, right(dqkv, 0, 3, j)) * 0.5
    grad_out[...] = dot_tn(left(dy, dy_oth), right(xn_ctx, half, 1, 0)) * 0.5


def grad_call(sc, xn_ctx, xn_oth, dy, dy_oth, dqkv, wide):
    half = xn_oth.shape[1]
    step = 256
    items = (*xn_ctx, xn_oth, *dy, dy_oth, *dqkv)
    return pl.pallas_call(
        grad_kernel,
        grid=(half // step,),
        out_shape=[
            jax.ShapeDtypeStruct((3, half, wide), F32),
            jax.ShapeDtypeStruct((half, wide), F32),
        ],
        in_specs=[SM] + [pl.BlockSpec(a.shape, lambda i: (0, 0)) for a in items],
        out_specs=[
            pl.BlockSpec((3, step, wide), lambda i: (0, i, 0)),
            pl.BlockSpec((step, wide), lambda i: (i, 0)),
        ],
        compiler_params=pltpu.CompilerParams(vmem_limit_bytes=VMEM_LIMIT),
        name="grad",
    )(sc, *items)


def doc_mask(doc_lengths, row_count):
    doc_ends = jnp.cumsum(doc_lengths)
    places = jnp.arange(row_count, dtype=jnp.int32)
    segment = jnp.sum((places[:, None] >= doc_ends[None, :]).astype(jnp.int32), axis=1)
    return (segment[:, None] == segment[None, :]) & (places[None, :] <= places[:, None])


def in_pieces(x, z, c):
    halves = []
    for half in (c, 1 - c):
        halves.append(
            jnp.concatenate(
                [
                    lax.dynamic_slice_in_dim(x, 64 * half + 16 * lax.rem(z + 4 - k, 4), 16, 0)
                    for k in SHIFTS
                ],
                axis=0,
            )
        )
    return halves[0], halves[1], halves[0][:16]


def mean(x):
    return jnp.mean(x, axis=-1, keepdims=True)


def local(inputs, cotangent, lengths, down_qkv, down_out, down_gain, up_qkv, up_out, up_gain):
    place = lax.axis_index("pipe")
    tensor = lax.axis_index("tensor")
    z, c = tensor // 2, tensor % 2
    rows, width = inputs.shape[1], inputs.shape[2]
    wide = down_out.shape[2]
    weights = (
        jnp.transpose(down_qkv[0], (1, 0, 2)),
        jnp.transpose(up_qkv[0], (1, 0, 2)),
        down_out[0],
        up_out[0],
    )
    gain = jnp.concatenate([down_gain, up_gain], axis=0).astype(F32)
    allowed = jnp.stack([doc_mask(lengths[r, 0], rows) for r in range(2)]).astype(F32)

    def after(value, *others):
        return lax.optimization_barrier((value,) + others)[0]

    def scalars(is_down, is_up):
        active = (is_down | is_up).astype(jnp.int32)
        return jnp.stack([active, is_up.astype(jnp.int32), c, z]).astype(jnp.int32)

    state = alloc(
        [
            ((2, rows, width), BF16),
            ((2, 3, rows, wide), BF16),
            ((2, 3, rows, rows), F32),
            ((2, rows // 2, 2 * wide), BF16),
        ]
    )
    dy_state, dqkv_state = alloc([((2, rows, width), BF16), ((2, rows // 2, 6 * wide), BF16)])

    own, oth, block = in_pieces(jnp.where(place == 0, inputs[0], inputs[1]), z, c)
    kept = [block, block]
    for t in range(8):
        is_down, is_up = place == t, place == 7 - t
        sc = scalars(is_down, is_up)
        kept = [jnp.where(is_down, block, kept[0]), jnp.where(is_up, block, kept[1])]
        if t < 7:
            keep, send, *state = front_call(False, sc, own, oth, gain, allowed, weights, state)
            total = sum_over_tensor(keep, send, z)
            result = (block.astype(F32) + total).astype(BF16)
            own, oth, block = hop_and_spread(result, t)
        else:
            state = front_call(True, sc, own, oth, gain, allowed, weights, state)
    xn, qkv, prob, ctx = state
    b = lax.axis_index("dp")

    half = width // 2

    def features(a, which, core):
        return lax.dynamic_slice(a, (64 * core, which * half), (64, half))

    def other_halves(local_whole, items):
        received = other_core(jnp.concatenate([a[:, :half] for a in items[1:]], axis=0))
        return jnp.concatenate([features(local_whole, b, 1 - c), received], axis=0)

    xn_ctx = gather_items(
        lambda d, which: jnp.concatenate([features(xn[d], which, c), ctx[d]], axis=1), b
    )
    xn_oth = other_halves(xn[0], xn_ctx)

    x = jnp.stack(kept).astype(F32)
    xc = x - mean(x)
    rstd = lax.rsqrt(mean(xc * xc) + EPS)
    xhat = xc * rstd

    def tokens(own, oth):
        first, second = jnp.where(c == 0, own, oth), jnp.where(c == 0, oth, own)
        turned = jnp.concatenate([first, second], axis=0).reshape(2, 4, 16, width)
        order = [lax.rem(z + 4 - k, 4) for k in SHIFTS]
        blocks = [turned[:, 0]] * 4
        for place_to in range(4):
            for i in range(4):
                blocks[place_to] = jnp.where(order[i] == place_to, turned[:, i], blocks[place_to])
        return jnp.stack(blocks, axis=1).reshape(rows, width)

    own, oth, block = in_pieces(jnp.where(place == 7, cotangent[0], cotangent[1]), z, c)
    for t in range(8):
        is_down, is_up = place == 7 - t, place == t
        sc = scalars(is_down, is_up)
        if t < 7:
            keep, send, dy_state, dqkv_state = back_call(
                False, sc, own, oth, weights, qkv, prob, dy_state, dqkv_state
            )
            dxn = sum_over_tensor(keep, send, z)
            xhat_d = jnp.where(is_down, xhat[0], xhat[1])
            rstd_d = jnp.where(is_down, rstd[0], rstd[1])
            gr = dxn * jnp.where(is_down, gain[0:1], gain[1:2])
            change = rstd_d * (gr - mean(gr) - xhat_d * mean(gr * xhat_d))
            result = (block.astype(F32) + change).astype(BF16)
            own, oth, block = hop_and_spread(result, t)
            if t == 1:
                own, oth, block, xn_oth, *xn_ctx = lax.optimization_barrier(
                    (own, oth, block, xn_oth, *xn_ctx)
                )
        else:
            dy_now = [
                jnp.where(here, tokens(own, oth), dy_state[d])
                for d, here in enumerate((is_down, is_up))
            ]
            dy = gather_items(lambda d, which: features(dy_now[d], which, c), b)
            dy_oth = other_halves(dy_now[0], dy)
            dy_state, dqkv_state = back_call(
                True, sc, own, oth, weights, qkv, prob, dy_state, dqkv_state
            )

    dqkv = gather_items(lambda d, which: dqkv_state[d], b)
    grad_qkv, grad_out = grad_call(sc, xn_ctx, xn_oth, dy, dy_oth, dqkv, wide)
    return jnp.transpose(grad_qkv, (1, 0, 2))[None], grad_out[None]


def solution(mesh):
    placed = (
        P(None, "dp", None),
        P(None, "dp", None),
        P(None, "dp", None),
        P("pipe", None, None, "tensor"),
        P("pipe", None, "tensor"),
        P("pipe", None),
        P("pipe", None, None, "tensor"),
        P("pipe", None, "tensor"),
        P("pipe", None),
    )
    return jax.shard_map(
        local,
        mesh=mesh,
        in_specs=placed,
        out_specs=(P("pipe", "dp", None, "tensor"), P("pipe", "dp", "tensor")),
        check_vma=False,
    )
```

```python
import functools
import jax
import jax.numpy as jnp
from jax import lax
from jax.experimental import pallas as pl
from jax.experimental.pallas import tpu as pltpu
from jax.sharding import PartitionSpec as P

HS = 128
EPS = 1e-05
FACTOR = HS ** (-0.5)
F32 = jnp.float32
BF16 = jnp.bfloat16
SHIFTS = (0, 1, 3, 2)
WEIGHT_PARTS = 2
VMEM_LIMIT = 24 * 1024 * 1024


def dot_nn(a, b):
    return lax.dot_general(a, b, (((1,), (0,)), ((), ())), preferred_element_type=F32)


def dot_nt(a, b):
    return lax.dot_general(a, b, (((1,), (1,)), ((), ())), preferred_element_type=F32)


def dot_tn(a, b):
    return lax.dot_general(a, b, (((0,), (0,)), ((), ())), preferred_element_type=F32)


def piece_rows(z, i, half):
    return pl.multiple_of(64 * half + 16 * lax.rem(z + 4 - SHIFTS[i], 4), 16)


def start_weights(d, down, up, held, sems):
    for choice, refs in ((0, down), (1, up)):

        @pl.when(d == choice)
        def _():
            for n, (source, target) in enumerate(zip(refs, held)):
                size = source.shape[0] // WEIGHT_PARTS
                for m in range(WEIGHT_PARTS):
                    part = pl.ds(m * size, size)
                    pltpu.make_async_copy(source.at[part], target.at[part], sems.at[n]).start()


def wait_weights(n, source, target, sems):
    pltpu.make_async_copy(source, target, sems.at[n]).wait()


def front_kernel(
    last, sc, own, oth, gain, allowed, wd, wu, od, ou, xn_i, qkv_i, prob_i, ctx_i, *refs
):
    if last:
        xn_o, qkv_o, prob_o, ctx_o, w, o, xn, qkv, prob, ctx, wsem, ssem = refs
    else:
        keep, send, xn_o, qkv_o, prob_o, ctx_o, w, o, xn, qkv, prob, ctx, wsem, ssem = refs
    active, d, c, z = sc[0], sc[1], sc[2], sc[3]

    @pl.when(active == 1)
    def _():
        held = [w.at[0], w.at[1], w.at[2]] + ([] if last else [o])
        down = [wd.at[0], wd.at[1], wd.at[2]] + ([] if last else [od])
        up = [wu.at[0], wu.at[1], wu.at[2]] + ([] if last else [ou])
        start_weights(d, down, up, held, wsem)
        g = gain[pl.ds(d, 1), :]
        for ref, half in ((own, c), (oth, 1 - c)):
            for i in range(4):
                x = ref[16 * i : 16 * i + 16, :].astype(F32)
                xc = x - jnp.mean(x, axis=-1, keepdims=True)
                rstd = lax.rsqrt(jnp.mean(xc * xc, axis=-1, keepdims=True) + EPS)
                xn[pl.ds(piece_rows(z, i, half), 16), :] = (xc * rstd * g).astype(BF16)
        copies = [pltpu.make_async_copy(xn, xn_o.at[d], ssem.at[0])]
        copies[0].start()
        for j in range(3):
            wait_weights(j, down[j], held[j], wsem)
            qkv[j] = dot_nn(xn[...], w[j]).astype(BF16)
        copies.append(pltpu.make_async_copy(qkv, qkv_o.at[d], ssem.at[1]))
        copies[1].start()
        mask = allowed[d] > 0.5
        for h in range(3):
            cols = slice(h * HS, h * HS + HS)
            s = dot_nt(qkv[0, :, cols], qkv[1, :, cols]) * FACTOR
            s = jnp.where(mask, s, -1e30)
            e = jnp.exp(s - jnp.max(s, axis=-1, keepdims=True))
            p = e / jnp.sum(e, axis=-1, keepdims=True)
            prob[h] = p
            ctx_h = dot_nn(p.astype(BF16), qkv[2, :, cols]).astype(BF16)
            for side in range(2):
                at = side * 3 * HS + h * HS
                ctx[:, at : at + HS] = ctx_h[64 * side : 64 * side + 64]
        copies.append(pltpu.make_async_copy(prob, prob_o.at[d], ssem.at[2]))
        copies.append(pltpu.make_async_copy(ctx, ctx_o.at[d], ssem.at[3]))
        copies[2].start()
        copies[3].start()
        if not last:
            lhs = jnp.concatenate(
                [
                    ctx[:, pl.ds(pl.multiple_of(side * 3 * HS, HS), 3 * HS)]
                    for side in (1 - c, c)
                ],
                axis=0,
            )
            wait_weights(3, od, o, wsem)
            for n in range(5):
                cols = slice(512 * n, 512 * n + 512)
                part = dot_nt(lhs, o[cols, :]).astype(BF16)
                send[:, cols] = part[:64]
                keep[:, cols] = part[64:]
        for copy in copies:
            copy.wait()


def back_kernel(last, sc, own, oth, wd, wu, od, ou, qkv_i, prob_i, dy_i, dqkv_i, *refs):
    if last:
        dy_o, dqkv_o, w, o, dy, qkv, prob, dqkv, grads, wsem, ssem = refs
    else:
        keep, send, dy_o, dqkv_o, w, o, dy, qkv, prob, dqkv, grads, wsem, ssem = refs
    active, d, c, z = sc[0], sc[1], sc[2], sc[3]

    @pl.when(active == 1)
    def _():
        held = [o] + ([] if last else [w.at[0], w.at[1], w.at[2]])
        down = [od] + ([] if last else [wd.at[0], wd.at[1], wd.at[2]])
        up = [ou] + ([] if last else [wu.at[0], wu.at[1], wu.at[2]])
        loads = [
            pltpu.make_async_copy(qkv_i.at[d], qkv, ssem.at[0]),
            pltpu.make_async_copy(prob_i.at[d], prob, ssem.at[1]),
        ]
        for load in loads:
            load.start()
        start_weights(d, down, up, held, wsem)
        for ref, half in ((own, c), (oth, 1 - c)):
            for i in range(4):
                dy[pl.ds(piece_rows(z, i, half), 16), :] = ref[16 * i : 16 * i + 16, :]
        copies = [pltpu.make_async_copy(dy, dy_o.at[d], ssem.at[2])]
        copies[0].start()
        wait_weights(0, od, o, wsem)
        dctx = dot_nn(dy[...], o[...]).astype(BF16)
        for load in loads:
            load.wait()
        for h in range(3):
            cols = slice(h * HS, h * HS + HS)
            p = prob[h]
            dctx_h = dctx[:, cols]
            dp = dot_nt(dctx_h, qkv[2, :, cols])
            inner = jnp.sum(p * dp, axis=-1, keepdims=True)
            ds = (p * (dp - inner) * FACTOR).astype(BF16)
            grads[0, :, cols] = dot_nn(ds, qkv[1, :, cols]).astype(BF16)
            grads[1, :, cols] = dot_tn(ds, qkv[0, :, cols]).astype(BF16)
            grads[2, :, cols] = dot_tn(p.astype(BF16), dctx_h).astype(BF16)
        for j in range(3):
            for side in range(2):
                at = (side * 3 + j) * 3 * HS
                dqkv[:, at : at + 3 * HS] = grads[j, 64 * side : 64 * side + 64, :]
        copies.append(pltpu.make_async_copy(dqkv, dqkv_o.at[d], ssem.at[3]))
        copies[1].start()
        if not last:
            lhs = []
            for j in range(3):
                lhs.append(
                    jnp.concatenate(
                        [
                            grads[j, pl.ds(pl.multiple_of(64 * side, 64), 64), :]
                            for side in (1 - c, c)
                        ],
                        axis=0,
                    )
                )
            for j in range(3):
                wait_weights(1 + j, wd.at[j], w.at[j], wsem)
            for n in range(5):
                cols = slice(512 * n, 512 * n + 512)
                part = dot_nt(lhs[0], w[0, cols, :])
                part += dot_nt(lhs[1], w[1, cols, :])
                part += dot_nt(lhs[2], w[2, cols, :])
                part = part.astype(BF16)
                send[:, cols] = part[:64]
                keep[:, cols] = part[64:]
        for copy in copies:
            copy.wait()


ANY = pl.BlockSpec(memory_space=pltpu.HBM)
VM = pl.BlockSpec(memory_space=pltpu.VMEM)
SM = pl.BlockSpec(memory_space=pltpu.SMEM)


def like(a):
    return pltpu.HBM(a.shape, a.dtype)


def in_hbm(arrays):
    return [pltpu.with_memory_space_constraint(a, pltpu.HBM) for a in arrays]


def spread_like(rows, width):
    return jax.ShapeDtypeStruct((rows, width), BF16)


def front_call(last, sc, own, oth, gain, allowed, weights, state):
    rows, width = own.shape
    wide = weights[2].shape[1]
    xn, qkv, prob, ctx = state
    halves = [] if last else [spread_like(rows, width)] * 2
    first = len(halves)
    return pl.pallas_call(
        functools.partial(front_kernel, last),
        out_shape=halves + [like(a) for a in state],
        in_specs=[SM, VM, VM, VM, VM] + [ANY] * 8,
        out_specs=[VM] * first + [ANY] * 4,
        input_output_aliases={9 + n: first + n for n in range(4)},
        scratch_shapes=[
            pltpu.VMEM((3, width, wide), BF16),
            pltpu.VMEM((width, wide), BF16),
            pltpu.VMEM(xn.shape[1:], BF16),
            pltpu.VMEM(qkv.shape[1:], BF16),
            pltpu.VMEM(prob.shape[1:], F32),
            pltpu.VMEM(ctx.shape[1:], BF16),
            pltpu.SemaphoreType.DMA((4,)),
            pltpu.SemaphoreType.DMA((4,)),
        ],
        compiler_params=pltpu.CompilerParams(vmem_limit_bytes=VMEM_LIMIT),
        cost_estimate=pl.CostEstimate(
            flops=2 * 128 * width * wide * 4, bytes_accessed=8 * width * wide, transcendentals=0
        ),
        name="front",
    )(sc, own, oth, gain, allowed, *in_hbm((*weights, *state)))


def back_call(last, sc, own, oth, weights, qkv, prob, dy, dqkv):
    rows, width = own.shape
    wide = weights[2].shape[1]
    halves = [] if last else [spread_like(rows, width)] * 2
    first = len(halves)
    return pl.pallas_call(
        functools.partial(back_kernel, last),
        out_shape=halves + [like(dy), like(dqkv)],
        in_specs=[SM, VM, VM] + [ANY] * 8,
        out_specs=[VM] * first + [ANY] * 2,
        input_output_aliases={9: first, 10: first + 1},
        scratch_shapes=[
            pltpu.VMEM((3, width, wide), BF16),
            pltpu.VMEM((width, wide), BF16),
            pltpu.VMEM(dy.shape[1:], BF16),
            pltpu.VMEM(qkv.shape[1:], BF16),
            pltpu.VMEM(prob.shape[1:], F32),
            pltpu.VMEM(dqkv.shape[1:], BF16),
            pltpu.VMEM(qkv.shape[1:], BF16),
            pltpu.SemaphoreType.DMA((4,)),
            pltpu.SemaphoreType.DMA((4,)),
        ],
        compiler_params=pltpu.CompilerParams(vmem_limit_bytes=VMEM_LIMIT),
        cost_estimate=pl.CostEstimate(
            flops=2 * 128 * width * wide * 4, bytes_accessed=8 * width * wide, transcendentals=0
        ),
        name="back",
    )(sc, own, oth, *in_hbm((*weights, qkv, prob, dy, dqkv)))


def alloc_kernel(*refs):
    pass


def alloc(shapes):
    return pl.pallas_call(
        alloc_kernel,
        out_shape=[pltpu.HBM(s, t) for s, t in shapes],
        out_specs=[ANY] * len(shapes),
        name="alloc",
    )()


def stage_partner(t, p):
    if t % 2 == 0:
        return p ^ 1
    if t == 3:
        return (7, 2, 1, 4, 3, 6, 5, 0)[p]
    return (3, 2, 1, 0, 7, 6, 5, 4)[p]


AXES = ("pipe", "tensor")


def permute(x, target):
    pairs = []
    for p in range(8):
        for z in range(4):
            for c in range(2):
                tp, tz, tc = target(p, z, c)
                pairs.append((p * 8 + z * 2 + c, tp * 8 + tz * 2 + tc))
    return lax.ppermute(x, AXES, pairs)


def other_core(x):
    return permute(x, lambda p, z, c: (p, z, 1 - c))


def sum_over_tensor(keep, send, z):
    pair = (keep.astype(F32) + other_core(send).astype(F32)).astype(BF16)
    parts = []
    for k in (2, 1, 3):
        block = lax.dynamic_slice_in_dim(pair, 16 * lax.rem(z + k, 4), 16, 0)
        parts.append(permute(block, lambda p, zz, c: (p, (zz + k) % 4, c)))
    own = lax.dynamic_slice_in_dim(pair, 16 * z, 16, 0)
    return own.astype(F32) + parts[0].astype(F32) + parts[1].astype(F32) + parts[2].astype(F32)


def hop_and_spread(block, t):
    pieces = [
        permute(block, lambda p, z, c: (stage_partner(t, p), (z + k) % 4, c)) for k in SHIFTS
    ]
    own = jnp.concatenate(pieces, axis=0)
    return own, other_core(own), pieces[0]


def mirror(a, flip):
    pairs = [(p * 2 + b, (7 - p) * 2 + (b ^ flip)) for b in range(2) for p in range(8)]
    return lax.ppermute(a, ("pipe", "dp"), pairs)


def swap_dp(a):
    return lax.ppermute(a, "dp", [(0, 1), (1, 0)])


def gather_items(pick, b):
    return [
        pick(0, b),
        swap_dp(pick(0, 1 - b)),
        mirror(pick(1, b), 0),
        mirror(pick(1, 1 - b), 1),
    ]


def grad_kernel(sc, *refs):
    xn_ctx, xn_oth, dy, dy_oth, dqkv = refs[0:4], refs[4], refs[5:9], refs[9], refs[10:14]
    grad_qkv, grad_out = refs[14:]
    step, wide = grad_out.shape
    half = xn_oth.shape[1]
    c = sc[2]
    rows = pl.ds(pl.multiple_of(pl.program_id(0) * step, step), step)

    def left(items, others):
        return jnp.concatenate([r[:, rows] for r in items] + [others[:, rows]], axis=0)

    def right(items, base, count, j):
        starts = [base + side * count * wide + j * wide for side in (c, 1 - c)]
        return jnp.concatenate(
            [r[:, pl.ds(pl.multiple_of(start, 128), wide)] for start in starts for r in items],
            axis=0,
        )

    lhs = left(xn_ctx, xn_oth)
    for j in range(3):
        grad_qkv[j] = dot_tn(lhs, right(dqkv, 0, 3, j)) * 0.5
    grad_out[...] = dot_tn(left(dy, dy_oth), right(xn_ctx, half, 1, 0)) * 0.5


def grad_call(sc, xn_ctx, xn_oth, dy, dy_oth, dqkv, wide):
    half = xn_oth.shape[1]
    step = 256
    items = (*xn_ctx, xn_oth, *dy, dy_oth, *dqkv)
    return pl.pallas_call(
        grad_kernel,
        grid=(half // step,),
        out_shape=[
            jax.ShapeDtypeStruct((3, half, wide), F32),
            jax.ShapeDtypeStruct((half, wide), F32),
        ],
        in_specs=[SM] + [pl.BlockSpec(a.shape, lambda i: (0, 0)) for a in items],
        out_specs=[
            pl.BlockSpec((3, step, wide), lambda i: (0, i, 0)),
            pl.BlockSpec((step, wide), lambda i: (i, 0)),
        ],
        compiler_params=pltpu.CompilerParams(vmem_limit_bytes=VMEM_LIMIT),
        name="grad",
    )(sc, *items)


def doc_mask(doc_lengths, row_count):
    doc_ends = jnp.cumsum(doc_lengths)
    places = jnp.arange(row_count, dtype=jnp.int32)
    segment = jnp.sum((places[:, None] >= doc_ends[None, :]).astype(jnp.int32), axis=1)
    return (segment[:, None] == segment[None, :]) & (places[None, :] <= places[:, None])


def in_pieces(x, z, c):
    halves = []
    for half in (c, 1 - c):
        halves.append(
            jnp.concatenate(
                [
                    lax.dynamic_slice_in_dim(x, 64 * half + 16 * lax.rem(z + 4 - k, 4), 16, 0)
                    for k in SHIFTS
                ],
                axis=0,
            )
        )
    return halves[0], halves[1], halves[0][:16]


def mean(x):
    return jnp.mean(x, axis=-1, keepdims=True)


def local(inputs, cotangent, lengths, down_qkv, down_out, down_gain, up_qkv, up_out, up_gain):
    place = lax.axis_index("pipe")
    tensor = lax.axis_index("tensor")
    z, c = tensor // 2, tensor % 2
    rows, width = inputs.shape[1], inputs.shape[2]
    wide = down_out.shape[2]
    weights = (
        jnp.transpose(down_qkv[0], (1, 0, 2)),
        jnp.transpose(up_qkv[0], (1, 0, 2)),
        down_out[0],
        up_out[0],
    )
    gain = jnp.concatenate([down_gain, up_gain], axis=0).astype(F32)
    allowed = jnp.stack([doc_mask(lengths[r, 0], rows) for r in range(2)]).astype(F32)

    def after(value, *others):
        return lax.optimization_barrier((value,) + others)[0]

    def scalars(is_down, is_up):
        active = (is_down | is_up).astype(jnp.int32)
        return jnp.stack([active, is_up.astype(jnp.int32), c, z]).astype(jnp.int32)

    state = alloc(
        [
            ((2, rows, width), BF16),
            ((2, 3, rows, wide), BF16),
            ((2, 3, rows, rows), F32),
            ((2, rows // 2, 2 * wide), BF16),
        ]
    )
    dy_state, dqkv_state = alloc([((2, rows, width), BF16), ((2, rows // 2, 6 * wide), BF16)])

    own, oth, block = in_pieces(jnp.where(place == 0, inputs[0], inputs[1]), z, c)
    kept = [block, block]
    for t in range(8):
        is_down, is_up = place == t, place == 7 - t
        sc = scalars(is_down, is_up)
        kept = [jnp.where(is_down, block, kept[0]), jnp.where(is_up, block, kept[1])]
        if t < 7:
            keep, send, *state = front_call(False, sc, own, oth, gain, allowed, weights, state)
            total = sum_over_tensor(keep, send, z)
            result = (block.astype(F32) + total).astype(BF16)
            own, oth, block = hop_and_spread(result, t)
        else:
            state = front_call(True, sc, own, oth, gain, allowed, weights, state)
    xn, qkv, prob, ctx = state
    b = lax.axis_index("dp")

    half = width // 2

    def features(a, which, core):
        return lax.dynamic_slice(a, (64 * core, which * half), (64, half))

    def other_halves(local_whole, items):
        received = other_core(jnp.concatenate([a[:, :half] for a in items[1:]], axis=0))
        return jnp.concatenate([features(local_whole, b, 1 - c), received], axis=0)

    xn_ctx = gather_items(
        lambda d, which: jnp.concatenate([features(xn[d], which, c), ctx[d]], axis=1), b
    )
    xn_oth = other_halves(xn[0], xn_ctx)

    x = jnp.stack(kept).astype(F32)
    xc = x - mean(x)
    rstd = lax.rsqrt(mean(xc * xc) + EPS)
    xhat = xc * rstd

    def tokens(own, oth):
        first, second = jnp.where(c == 0, own, oth), jnp.where(c == 0, oth, own)
        turned = jnp.concatenate([first, second], axis=0).reshape(2, 4, 16, width)
        order = [lax.rem(z + 4 - k, 4) for k in SHIFTS]
        blocks = [turned[:, 0]] * 4
        for place_to in range(4):
            for i in range(4):
                blocks[place_to] = jnp.where(order[i] == place_to, turned[:, i], blocks[place_to])
        return jnp.stack(blocks, axis=1).reshape(rows, width)

    own, oth, block = in_pieces(jnp.where(place == 7, cotangent[0], cotangent[1]), z, c)
    for t in range(8):
        is_down, is_up = place == 7 - t, place == t
        sc = scalars(is_down, is_up)
        if t < 7:
            keep, send, dy_state, dqkv_state = back_call(
                False, sc, own, oth, weights, qkv, prob, dy_state, dqkv_state
            )
            dxn = sum_over_tensor(keep, send, z)
            xhat_d = jnp.where(is_down, xhat[0], xhat[1])
            rstd_d = jnp.where(is_down, rstd[0], rstd[1])
            gr = dxn * jnp.where(is_down, gain[0:1], gain[1:2])
            change = rstd_d * (gr - mean(gr) - xhat_d * mean(gr * xhat_d))
            result = (block.astype(F32) + change).astype(BF16)
            own, oth, block = hop_and_spread(result, t)
            if t == 1:
                own, oth, block, xn_oth, *xn_ctx = lax.optimization_barrier(
                    (own, oth, block, xn_oth, *xn_ctx)
                )
        else:
            dy_now = [
                jnp.where(here, tokens(own, oth), dy_state[d])
                for d, here in enumerate((is_down, is_up))
            ]
            dy = gather_items(lambda d, which: features(dy_now[d], which, c), b)
            dy_oth = other_halves(dy_now[0], dy)
            dy_state, dqkv_state = back_call(
                True, sc, own, oth, weights, qkv, prob, dy_state, dqkv_state
            )

    dqkv = gather_items(lambda d, which: dqkv_state[d], b)
    grad_qkv, grad_out = grad_call(sc, xn_ctx, xn_oth, dy, dy_oth, dqkv, wide)
    return jnp.transpose(grad_qkv, (1, 0, 2))[None], grad_out[None]


def solution(mesh):
    placed = (
        P(None, "dp", None),
        P(None, "dp", None),
        P(None, "dp", None),
        P("pipe", None, None, "tensor"),
        P("pipe", None, "tensor"),
        P("pipe", None),
        P("pipe", None, None, "tensor"),
        P("pipe", None, "tensor"),
        P("pipe", None),
    )
    return jax.shard_map(
        local,
        mesh=mesh,
        in_specs=placed,
        out_specs=(P("pipe", "dp", None, "tensor"), P("pipe", "dp", "tensor")),
        check_vma=False,
    )
```
